128 devices in a mesh: seq: 32 (over y, x, core), vis: 4 (over z).
Axes of the slice: x: 4, y: 4, z: 4, core: 2. Of those that a mesh axis runs over, the one named last changes fastest.
Arguments:
- queries: bfloat16 [65536, 4096], P('seq', 'vis'), may hold values from -8 to 8
- latent_keys: bfloat16 [256, 64, 4096], P('seq', 'vis'), may hold values from -6 to 6
- latent_values: bfloat16 [256, 64, 4096], P('seq', 'vis'), may hold values from -6 to 6
- gate_vector: float32 [4096], P('vis'), may hold values from -1.2 to 1.2
- cotangent: bfloat16 [65536, 4096], P('seq', 'vis'), may hold values from -48 to 48
- image_slot: int32 [256], replicated, may hold values from 0 to 255, as said below
- image_lists: int32 [128, 12], replicated, may hold values from 0 to 255, as said below
Outputs:
- gated_output: bfloat16 [65536, 4096], P('seq', 'vis')
- grad_queries: bfloat16 [65536, 4096], P('seq', 'vis')
- grad_keys: bfloat16 [256, 64, 4096], P('seq', 'vis')
- grad_values: bfloat16 [256, 64, 4096], P('seq', 'vis')
- grad_gate: float32 [4096], P('vis')
The draws below stay inside these ranges and needn't reach their ends.
Inputs may be any that keep to these rules, and one draw needn't show every extreme that they name: A permutation: image i, of document i // 32, is stored at slot image_slot[i], that is on index image_slot[i] // 8 of seq; every index of seq stores exactly one image of each of the 8 documents and no others. `image_lists`: row b names 12 distinct images, all of the document of block b, that is ids d * 32 to (d + 1) * 32 - 1 with d = b * 512 // 8192; the 4 blocks of each aligned run of 2048 tokens together name every one of the 32 images of their document (possible since 12 * 4 >= 32).
All inputs are finite; a program needn't handle non-finite values.
Results may differ from the reference program's by a relative error of at most 0.0099.
Values may be sent and summed in bfloat16 or wider, within the bound.
A program may use at most 256 MiB of HBM per device.

```python
import math
import jax
import jax.numpy as jnp
from jax import lax

HEADS = 32
HD = 128
LAT = 64
IMG_DOC = 32
DOC_TOK = 8192
BLK = 512
ATT = 12
TOK_DEV = 2048
TOKENS = 65536
HW = 4096
DOCS = 8
IMAGES = 256
IMG_DEV = 8
CAP = 1
NBLK = 128


def doc_order(sub_key):
    return jax.random.permutation(sub_key, IMG_DOC).astype(jnp.int32)


def doc_place(sub_key):
    return jax.random.permutation(sub_key, DOCS).astype(jnp.int32)


def draw_queries(key, part):
    key = jax.random.fold_in(key, 7)
    base_key = jax.random.fold_in(key, 0)
    base_draw = jnp.clip(jax.random.normal(base_key, (TOKENS, HW), jnp.float32), -6.0, 6.0)
    return base_draw.astype(jnp.bfloat16)


def draw_latent_keys(key, part):
    key = jax.random.fold_in(key, 5)
    base_key = jax.random.fold_in(key, 0)
    base_draw = jnp.clip(jax.random.normal(base_key, (IMAGES, LAT, HW), jnp.float32), -6.0, 6.0)
    return base_draw.astype(jnp.bfloat16)


def draw_cotangent(key, part):
    key = jax.random.fold_in(key, 13)
    base_key, spread_key = jax.random.split(key, 2)
    row_rise = 1.0 + 2.0 * jnp.arange(TOKENS, dtype=jnp.float32)[:, None] / (TOKENS - 1)
    spread = jnp.exp(jax.random.uniform(spread_key, (TOKENS, 1), jnp.float32, 0.0, 1.3862944))
    base_draw = jnp.clip(jax.random.normal(base_key, (TOKENS, HW), jnp.float32), -4.0, 4.0) * row_rise * spread
    return base_draw.astype(jnp.bfloat16)


def draw_image_slot(key, part):
    key = jax.random.fold_in(key, 3)
    order_key, place_key, owner_key = jax.random.split(key, 3)
    groups_doc = IMG_DOC // CAP
    groups_dev = IMG_DEV // CAP
    owners = IMAGES // IMG_DEV
    in_doc_order = jax.vmap(doc_order)(jax.random.split(order_key, DOCS))
    placed = jax.vmap(doc_place)(jax.random.split(place_key, groups_doc))
    owner_order = jax.random.permutation(owner_key, owners).astype(jnp.int32)
    doc_index = jnp.arange(DOCS, dtype=jnp.int32)[:, None, None]
    group_index = jnp.arange(groups_doc, dtype=jnp.int32)[None, :, None]
    member = jnp.arange(CAP, dtype=jnp.int32)[None, None, :]
    ranked = group_index * DOCS + placed.T[:, :, None] + 0 * member
    owner = owner_order[ranked // groups_dev]
    within = ranked % groups_dev * CAP + member
    slots = owner * IMG_DEV + within
    image_ids = doc_index * IMG_DOC + in_doc_order.reshape(DOCS, groups_doc, CAP)
    table = jnp.zeros((IMAGES,), jnp.int32).at[image_ids.reshape(-1)].set(slots.reshape(-1))
    return table


def draw_image_lists(key, part):
    key = jax.random.fold_in(key, 23)
    perm_key, step_key = jax.random.split(key)
    runs_total = TOKENS // TOK_DEV
    blocks_run = TOK_DEV // BLK
    step_low = min(ATT, max(1, -(-(IMG_DOC - ATT) // max(1, blocks_run - 1))))
    doc_perms = jax.vmap(doc_order)(jax.random.split(perm_key, runs_total))
    step_size = jax.random.randint(step_key, (runs_total,), step_low, ATT + 1).astype(jnp.int32)
    block_index = jnp.arange(blocks_run, dtype=jnp.int32)
    member = jnp.arange(ATT, dtype=jnp.int32)
    offsets = (block_index[None, :, None] * step_size[:, None, None] + member[None, None, :]) % IMG_DOC
    widened = jnp.broadcast_to(doc_perms[:, None, :], (runs_total, blocks_run, IMG_DOC))
    local_ids = jnp.take_along_axis(widened, offsets, axis=2)
    doc_index = jnp.arange(runs_total, dtype=jnp.int32) * TOK_DEV // DOC_TOK
    block_ids = doc_index[:, None, None] * IMG_DOC + local_ids
    return block_ids.reshape(NBLK, ATT).astype(jnp.int32)


def steps_of(key, shape, cuts, smallest, top_value):
    level, own = 1.0, jax.random.fold_in(key, 6)
    for axis_at, shards_of in cuts:
        steps = jnp.exp(jax.random.uniform(jax.random.fold_in(own, axis_at), (shards_of,), jnp.float32, smallest / len(cuts), top_value / len(cuts)))
        level = level * jnp.repeat(steps, shape[axis_at] // shards_of).reshape([-1 if axis == axis_at else 1 for axis in range(len(shape))])
    return level


def scatter_about(own_key, shape, deviation, reach, shards=(), held_as=jnp.bfloat16):
    entries = deviation * jax.random.normal(own_key, shape, jnp.float32)
    if shards:
        entries = entries * steps_of(own_key, shape, shards, -0.22, 0.18)
    return jnp.clip(entries, -reach, reach).astype(held_as)


def setup_inputs(seed: int = 0) -> dict:
    splits = jax.random.split(jax.random.key(seed), 8)
    queries = draw_queries(jax.random.fold_in(splits[7], 71), 0)
    latent_keys = draw_latent_keys(jax.random.fold_in(splits[7], 71), 0)
    latent_values = scatter_about(splits[2], (IMAGES, LAT, HW), 1.0, 6.0, ((0, 32), (1, 4)))
    gate_vector = jnp.clip(jax.random.uniform(splits[3], (HW,), jnp.float32, -1.2, 1.2) * steps_of(splits[3], (HW,), ((0, 4),), -0.4, 0.0), -1.2, 1.2)
    cotangent = draw_cotangent(jax.random.fold_in(splits[7], 71), 0)
    image_slot = draw_image_slot(jax.random.fold_in(splits[7], 71), 0)
    image_lists = draw_image_lists(jax.random.fold_in(splits[7], 71), 0)
    return dict(queries=queries, latent_keys=latent_keys, latent_values=latent_values, gate_vector=gate_vector, cotangent=cotangent, image_slot=image_slot, image_lists=image_lists)


def rounded(values_in):
    return lax.optimization_barrier(values_in.astype(jnp.bfloat16)).astype(jnp.float32)

def reference(queries, latent_keys, latent_values, gate_vector, cotangent, image_slot, image_lists):
    score_scale = 1.0 / math.sqrt(HD)
    tanh_gate = jnp.tanh(gate_vector)
    tanh_slope = 1.0 - tanh_gate * tanh_gate
    runs_total = TOKENS // TOK_DEV
    blocks_run = TOK_DEV // BLK

    def run_step(totals, run_index):
        sum_keys, sum_values, gate_total = totals
        row_start = run_index * TOK_DEV
        doc_index = row_start // DOC_TOK
        part_keys = jnp.zeros((IMG_DOC, LAT, HW), jnp.float32)
        part_values = jnp.zeros((IMG_DOC, LAT, HW), jnp.float32)
        gated_list = []
        query_list = []
        for inner_block in range(blocks_run):
            first_row = row_start + inner_block * BLK
            query_block = lax.dynamic_slice_in_dim(queries, first_row, BLK, 0).astype(jnp.float32).reshape(BLK, HEADS, HD)
            cot_block = lax.dynamic_slice_in_dim(cotangent, first_row, BLK, 0).astype(jnp.float32)
            block_ids = lax.dynamic_slice_in_dim(image_lists, run_index * blocks_run + inner_block, 1, 0)[0]
            block_slots = image_slot[block_ids]
            key_block = latent_keys[block_slots].astype(jnp.float32).reshape(ATT * LAT, HEADS, HD)
            value_block = latent_values[block_slots].astype(jnp.float32).reshape(ATT * LAT, HEADS, HD)
            scores = jnp.einsum('qhd,khd->hqk', query_block, key_block) * score_scale
            weights = jax.nn.softmax(scores, axis=2)
            weights_low = rounded(weights)
            attended = jnp.einsum('hqk,khd->qhd', weights_low, value_block)
            attended_flat = attended.reshape(BLK, HW)
            gated_list.append((tanh_gate * attended_flat).astype(jnp.bfloat16))
            gate_total = gate_total + lax.optimization_barrier(jnp.sum(cot_block * attended_flat * tanh_slope, axis=0))
            grad_attn = rounded(cot_block * tanh_gate).reshape(BLK, HEADS, HD)
            row_dot = lax.optimization_barrier(jnp.sum(grad_attn * attended, axis=2))
            grad_weights = jnp.einsum('qhd,khd->hqk', grad_attn, value_block)
            grad_scores = rounded(weights * (grad_weights - row_dot.T[:, :, None]) * score_scale)
            query_grad = jnp.einsum('hqk,khd->qhd', grad_scores, key_block).reshape(BLK, HW)
            query_list.append(query_grad.astype(jnp.bfloat16))
            key_term = jnp.einsum('hqk,qhd->khd', grad_scores, query_block).reshape(ATT, LAT, HW)
            value_term = jnp.einsum('hqk,qhd->khd', weights_low, grad_attn).reshape(ATT, LAT, HW)
            local_ids = block_ids - doc_index * IMG_DOC
            part_keys = part_keys.at[local_ids].add(key_term)
            part_values = part_values.at[local_ids].add(value_term)
        doc_slots = image_slot[doc_index * IMG_DOC + jnp.arange(IMG_DOC, dtype=jnp.int32)]
        sum_keys = sum_keys.at[doc_slots].add(rounded(part_keys))
        sum_values = sum_values.at[doc_slots].add(rounded(part_values))
        return ((sum_keys, sum_values, gate_total), (jnp.concatenate(gated_list, 0), jnp.concatenate(query_list, 0)))
    start_totals = (jnp.zeros((IMAGES, LAT, HW), jnp.float32), jnp.zeros((IMAGES, LAT, HW), jnp.float32), jnp.zeros((HW,), jnp.float32))
    totals, stacked = lax.scan(run_step, start_totals, jnp.arange(runs_total, dtype=jnp.int32))
    sum_keys, sum_values, gate_total = totals
    gated_output = stacked[0].reshape(TOKENS, HW)
    grad_queries = stacked[1].reshape(TOKENS, HW)
    return (gated_output, grad_queries, sum_keys.astype(jnp.bfloat16), sum_values.astype(jnp.bfloat16), gate_total)
```

```python
import math

import jax
import jax.numpy as jnp
from jax import lax
from jax.experimental import pallas as pl
from jax.experimental.pallas import tpu as pltpu
from jax.sharding import PartitionSpec as P

HD = 128
LAT = 64
PART = 16
DOC = 32
DOCS = 8
ATT = 12
BLK = 512
ROWS = 2048
HEADS = 4
BLOCKS = 8
HALF = HEADS * HD
KEYS = ATT * LAT
SCALE = 1.0 / math.sqrt(HD)
EXP_SCALE = math.log2(math.e) / math.sqrt(HD)
MESH = pl.DeviceIdType.MESH
f32, bf16, i32 = jnp.float32, jnp.bfloat16, jnp.int32


def contract_last(left, right):
    return lax.dot_general(left, right, (((1,), (1,)), ((), ())), preferred_element_type=f32)


def dot(left, right):
    return jnp.dot(left, right, preferred_element_type=f32)


def kernel(
    slot_ref, lists_ref, q_hbm, cot_hbm, lk, lv, gate_ref,
    out_hbm, gq_hbm, gk_out, gv_out, gate_out,
    own_slot, own_doc, inverse,
    z_send, z_recv, y_recv, x_recv, q_work, c_work, k_all, v_all, k_blk, v_blk,
    k_term, v_term, part, bx_recv, by_send, by_recv, bz_recv,
    g_part, g_x, g_row, g_y, g_all,
    zs, zr, ys, yr, xs, xr, bxs, bxr, bys, byr, bzs, bzr,
    til, tis, tir, tol, tos, tor, gxs, gxr, gys, gyr, gcs, gcr,
):
    seq = lax.axis_index("seq")
    z = lax.axis_index("vis")
    c = seq % 2
    x = (seq // 2) % 4
    y = seq // 8

    def at_z(k):
        return (y * 8 + x * 2 + (c + k) % 2, (z + k // 2) % 4)

    def at_y(k):
        return (((y + k) % 4) * 8 + x * 2 + c, z)

    def at_x(k):
        return (y * 8 + ((x + k) % 4) * 2 + c, z)

    sibling = at_z(1)

    def copy(src, dst, send, recv, device, k):
        if k == 0:
            return pltpu.make_async_copy(src, dst, recv)
        return pltpu.make_async_remote_copy(
            src_ref=src, dst_ref=dst, send_sem=send, recv_sem=recv, device_id=device, device_id_type=MESH
        )

    def z_copy(h, k):
        to = ((z + k // 2) % 4) * 2 + (c + k) % 2
        return copy(
            z_send.at[h, to], z_recv.at[h, :, c, :, pl.ds(pl.multiple_of(z * PART, PART), PART), :],
            zs.at[h, k], zr.at[h, k], at_z(k), k)

    def y_copy(h, k):
        return copy(
            z_recv.at[h, pl.ds(2 * ((y + k) % 4), 2)], y_recv.at[h, :, pl.ds(2 * y, 2)],
            ys.at[h, k], yr.at[h, k], at_y(k), k)

    def x_copy(h, k):
        return copy(
            y_recv.at[h, ((x + k) % 4) // 2], x_recv.at[h, pl.ds(x * 8, 8)],
            xs.at[h, k], xr.at[h, k], at_x(k), k)

    def bx_copy(h, k):
        return copy(
            part.at[h, pl.ds(((x + k) % 4) * 8, 8)], bx_recv.at[h, x],
            bxs.at[h, k], bxr.at[h, k], at_x(k), k)

    def by_copy(h, k):
        return copy(
            by_send.at[h, :, (y + k) % 4], by_recv.at[h, pl.ds(2 * y, 2)],
            bys.at[h, k], byr.at[h, k], at_y(k), k)

    def bz_copy(h, k):
        to_z = (z + k // 2) % 4
        return copy(
            by_recv.at[h, :, (c + k) % 2, :, pl.ds(pl.multiple_of(to_z * PART, PART), PART), :],
            bz_recv.at[h, z * 2 + c], bzs.at[h, k], bzr.at[h, k], at_z(k), k)

    def columns(half, h):
        return pl.ds(pl.multiple_of(half * HALF + h * HD, HD), HD)

    def text_local(h):
        return [
            pltpu.make_async_copy(src.at[:, columns(c, h)], dst.at[h, pl.ds(0, ROWS)], til.at[h, i])
            for i, (src, dst) in enumerate(((q_hbm, q_work), (cot_hbm, c_work)))]

    def text_remote(h):
        return [
            copy(src.at[:, columns(1 - c, h)], dst.at[h, pl.ds(ROWS, ROWS)],
                 tis.at[h, i], tir.at[h, i], sibling, 1)
            for i, (src, dst) in enumerate(((q_hbm, q_work), (cot_hbm, c_work)))]

    def result_local(h):
        return [
            pltpu.make_async_copy(src.at[h, pl.ds(0, ROWS)], dst.at[:, columns(c, h)], tol.at[h, i])
            for i, (src, dst) in enumerate(((q_work, gq_hbm), (c_work, out_hbm)))]

    def result_remote(h):
        return [
            copy(src.at[h, pl.ds(ROWS, ROWS)], dst.at[:, columns(c, h)],
                 tos.at[h, i], tor.at[h, i], sibling, 1)
            for i, (src, dst) in enumerate(((q_work, gq_hbm), (c_work, out_hbm)))]

    def start(copies):
        for one in copies:
            one.start()

    def arrive(make, h, count):
        make(h, 0).wait()
        for k in range(1, count):
            make(h, k).wait_recv()

    def sent(make, h, count):
        for k in range(1, count):
            make(h, k).wait_send()

    @pl.loop(0, HEADS)
    def _(h):
        start(text_local(h))

    barrier = pltpu.get_barrier_semaphore()
    partners = [at_z(k) for k in range(1, 8)] + [at_y(k) for k in range(1, 4)] + [at_x(k) for k in range(1, 4)]
    for one in partners:
        pl.semaphore_signal(barrier, inc=1, device_id=one, device_id_type=MESH)

    slots = []
    for d in range(DOCS):
        def look(i, found, d=d):
            at = slot_ref[d * DOC + i]
            return found + jnp.where(at // 8 == seq, at % 8, 0)
        slots.append(lax.fori_loop(0, DOC, look, jnp.int32(0), unroll=True))
        own_slot[d] = slots[d]
    for j in range(DOCS):
        doc = jnp.int32(0)
        for d in range(DOCS):
            doc = jnp.where(slots[d] == j, d, doc)
        own_doc[j] = doc

    @pl.loop(0, DOCS)
    def _(d):
        at = own_slot[d]
        for i, src in enumerate((lk, lv)):
            row = src[at]
            for to in range(8):
                for h in range(HEADS):
                    low = (to * HEADS + h) * HD
                    z_send[h, to, d, i] = row[:, low:low + HD]

    pl.semaphore_wait(barrier, len(partners))

    @pl.loop(0, HEADS)
    def _(h):
        for k in range(8):
            z_copy(h, k).start()

    @pl.loop(0, HEADS)
    def _(h):
        start(text_remote(h))

    def block_row(b):
        own = seq * 4 + b
        return jnp.where(b < 4, own, (seq + 1 - 2 * c) * 4 + b - 4)

    def place(b, a):
        owner = slot_ref[lists_ref[block_row(b), a]] // 8
        return ((owner // 2) % 4) * 8 + (owner // 8) * 2 + owner % 2

    @pl.loop(0, BLOCKS)
    def _(b):
        places = [place(b, a) for a in range(ATT)]

        @pl.loop(0, DOC)
        def _(p):
            found = jnp.int32(ATT)
            for a in range(ATT):
                found = jnp.where(places[a] == p, a, found)
            inverse[b, p] = found

    k_term[:, ATT] = jnp.zeros((BLOCKS, LAT, HD), f32)
    v_term[:, ATT] = jnp.zeros((BLOCKS, LAT, HD), f32)
    v_blk[:, HD:] = jnp.ones((KEYS, HD), bf16)
    g_part[...] = jnp.zeros((8, HD), f32)

    @pl.loop(0, HEADS + 1)
    def _(t):
        @pl.when(t < HEADS)
        def _():
            arrive(z_copy, t, 8)
            start([y_copy(t, k) for k in range(4)])

        @pl.when(t >= 1)
        def _():
            arrive(y_copy, t - 1, 4)
            start([x_copy(t - 1, k) for k in range(4)])

    def fold(h):
        arrive(bx_copy, h, 4)

        @pl.loop(0, 8)
        def _(i):
            for p in range(2):
                both = bx_recv[h, 2 * p, i].astype(f32) + bx_recv[h, 2 * p + 1, i].astype(f32)
                by_send[h, p, i // 2, i % 2] = both.astype(bf16)

        start([by_copy(h, k) for k in range(4)])

    def scatter(h):
        arrive(by_copy, h, 4)
        start([bz_copy(h, k) for k in range(8)])

    @pl.loop(0, HEADS)
    def _(h):
        arrive(x_copy, h, 4)
        for one in text_local(h):
            one.wait()
        for one in text_remote(h):
            one.wait_recv()
        k_all[...] = x_recv[h, :, 0]
        v_all[...] = x_recv[h, :, 1]
        gate = jnp.tanh(gate_ref[c * HEADS + h])

        def block(b, total):
            for a in range(ATT):
                at = place(b, a)
                k_blk[a * LAT:(a + 1) * LAT] = k_all[at]
                v_blk[a * LAT:(a + 1) * LAT, :HD] = v_all[at]
            keys = k_blk[...]
            values = v_blk[...]
            rows = pl.ds(pl.multiple_of(b * BLK, BLK), BLK)
            queries = q_work[h, rows]
            cot = c_work[h, rows].astype(f32)
            grad_attn = (cot * gate).astype(bf16)
            scores = contract_last(queries, keys)
            top = jnp.max(scores, axis=1, keepdims=True)
            raised = jnp.exp2((scores - top) * EXP_SCALE)
            raised_low = raised.astype(bf16)
            summed = dot(raised_low, values)
            share = 1.0 / summed[:, HD:]
            attended = summed[:, :HD] * share
            c_work[h, rows] = (attended * gate).astype(bf16)
            total = total + jnp.sum((cot * attended).reshape(BLK // 8, 8, HD), axis=0)
            row_dot = jnp.sum(grad_attn.astype(f32) * attended, axis=1, keepdims=True)
            grad_weights = contract_last(grad_attn, values[:, :HD])
            grad_scores = (raised * (grad_weights - row_dot)).astype(bf16)
            scaled = share * SCALE
            q_work[h, rows] = (dot(grad_scores, keys) * scaled).astype(bf16)
            query_share = (queries.astype(f32) * scaled).astype(bf16)
            grad_share = (grad_attn.astype(f32) * share).astype(bf16)
            k_term[b, :ATT] = dot(query_share.T, grad_scores).T.reshape(ATT, LAT, HD)
            v_term[b, :ATT] = dot(grad_share.T, raised_low).T.reshape(ATT, LAT, HD)
            return total

        total = lax.fori_loop(0, BLOCKS, block, jnp.zeros((8, HD), f32), unroll=UNROLL)
        g_part[pl.ds(h, 1)] = jnp.sum(total, axis=0, keepdims=True) * (1.0 - gate * gate)

        start(result_local(h))
        start(result_remote(h))

        @pl.loop(0, DOC)
        def _(p):
            key_sum = k_term[0, inverse[0, p]]
            value_sum = v_term[0, inverse[0, p]]
            for b in range(1, BLOCKS):
                key_sum = key_sum + k_term[b, inverse[b, p]]
                value_sum = value_sum + v_term[b, inverse[b, p]]
            part[h, p, 0] = key_sum.astype(bf16)
            part[h, p, 1] = value_sum.astype(bf16)

        start([bx_copy(h, k) for k in range(4)])

        @pl.when(h >= 1)
        def _():
            fold(h - 1)

        @pl.when(h >= 2)
        def _():
            scatter(h - 2)

    def gx_copy(k):
        return copy(g_part, g_x.at[x], gxs.at[k], gxr.at[k], at_x(k), k)

    def gy_copy(k):
        return copy(g_row, g_y.at[y], gys.at[k], gyr.at[k], at_y(k), k)

    def gc_copy(k):
        return copy(g_row, g_all.at[c], gcs.at[k], gcr.at[k], sibling, k)

    start([gx_copy(k) for k in range(4)])
    scatter(HEADS - 2)
    gx_copy(0).wait()
    for k in range(1, 4):
        gx_copy(k).wait()
    g_row[...] = (g_x[0] + g_x[1]) + (g_x[2] + g_x[3])
    start([gy_copy(k) for k in range(4)])
    fold(HEADS - 1)
    gy_copy(0).wait()
    for k in range(1, 4):
        gy_copy(k).wait()
    g_row[...] = (g_y[0] + g_y[1]) + (g_y[2] + g_y[3])
    start([gc_copy(k) for k in range(2)])
    scatter(HEADS - 1)
    gc_copy(0).wait()
    gc_copy(1).wait()
    for half in range(2):
        gate_out[half * HEADS:(half + 1) * HEADS] = g_all[half, :HEADS]

    @pl.loop(0, HEADS)
    def _(h):
        sent(z_copy, h, 8)
        sent(y_copy, h, 4)
        sent(x_copy, h, 4)
        sent(bx_copy, h, 4)
        sent(by_copy, h, 4)
        for one in text_remote(h):
            one.wait_send()
        for one in result_local(h):
            one.wait()
        for one in result_remote(h):
            one.wait()

    @pl.loop(0, HEADS)
    def _(h):
        arrive(bz_copy, h, 8)
        sent(bz_copy, h, 8)

    @pl.loop(0, DOCS)
    def _(j):
        d = own_doc[j]
        for h in range(HEADS):
            for source in range(8):
                low = (source * HEADS + h) * HD
                gk_out[j, :, low:low + HD] = bz_recv[h, source, d, 0]
                gv_out[j, :, low:low + HD] = bz_recv[h, source, d, 1]


UNROLL = 1


def local(queries, latent_keys, latent_values, gate_vector, cotangent, image_slot, image_lists):
    smem = pl.BlockSpec(memory_space=pltpu.SMEM)
    vmem = pl.BlockSpec(memory_space=pltpu.VMEM)
    hbm = pl.BlockSpec(memory_space=pl.ANY)
    dma = pltpu.SemaphoreType.DMA
    outs = pl.pallas_call(
        kernel,
        out_shape=[
            jax.ShapeDtypeStruct(queries.shape, bf16),
            jax.ShapeDtypeStruct(queries.shape, bf16),
            jax.ShapeDtypeStruct(latent_keys.shape, bf16),
            jax.ShapeDtypeStruct(latent_keys.shape, bf16),
            jax.ShapeDtypeStruct((2 * HEADS, HD), f32),
        ],
        in_specs=[smem, smem, hbm, hbm, vmem, vmem, vmem],
        out_specs=[hbm, hbm, vmem, vmem, vmem],
        scratch_shapes=[
            pltpu.SMEM((DOCS,), i32),
            pltpu.SMEM((DOCS,), i32),
            pltpu.SMEM((BLOCKS, DOC), i32),
            pltpu.VMEM((HEADS, 8, DOCS, 2, PART, HD), bf16),
            pltpu.VMEM((HEADS, DOCS, 2, 2, LAT, HD), bf16),
            pltpu.VMEM((HEADS, 2, 8, 2, LAT, HD), bf16),
            pltpu.VMEM((HEADS, DOC, 2, LAT, HD), bf16),
            pltpu.VMEM((HEADS, 2 * ROWS, HD), bf16),
            pltpu.VMEM((HEADS, 2 * ROWS, HD), bf16),
            pltpu.VMEM((DOC, LAT, HD), bf16),
            pltpu.VMEM((DOC, LAT, HD), bf16),
            pltpu.VMEM((KEYS, HD), bf16),
            pltpu.VMEM((KEYS, 2 * HD), bf16),
            pltpu.VMEM((BLOCKS, ATT + 1, LAT, HD), f32),
            pltpu.VMEM((BLOCKS, ATT + 1, LAT, HD), f32),
            pltpu.VMEM((HEADS, DOC, 2, LAT, HD), bf16),
            pltpu.VMEM((HEADS, 4, 8, 2, LAT, HD), bf16),
            pltpu.VMEM((HEADS, 2, 4, 2, 2, LAT, HD), bf16),
            pltpu.VMEM((HEADS, DOCS, 2, 2, LAT, HD), bf16),
            pltpu.VMEM((HEADS, 8, DOCS, 2, PART, HD), bf16),
            pltpu.VMEM((8, HD), f32),
            pltpu.VMEM((4, 8, HD), f32),
            pltpu.VMEM((8, HD), f32),
            pltpu.VMEM((4, 8, HD), f32),
            pltpu.VMEM((2, 8, HD), f32),
            dma((HEADS, 8)), dma((HEADS, 8)), dma((HEADS, 4)), dma((HEADS, 4)), dma((HEADS, 4)), dma((HEADS, 4)),
            dma((HEADS, 4)), dma((HEADS, 4)), dma((HEADS, 4)), dma((HEADS, 4)), dma((HEADS, 8)), dma((HEADS, 8)),
            dma((HEADS, 2)), dma((HEADS, 2)), dma((HEADS, 2)), dma((HEADS, 2)), dma((HEADS, 2)), dma((HEADS, 2)),
            dma((4,)), dma((4,)), dma((4,)), dma((4,)), dma((2,)), dma((2,)),
        ],
        compiler_params=pltpu.CompilerParams(
            collective_id=0, has_side_effects=True, vmem_limit_bytes=60 * 2**20
        ),
        name="attention",
    )(image_slot, image_lists, queries, cotangent, latent_keys, latent_values, gate_vector.reshape(2 * HEADS, 1, HD))
    gated, grad_queries, grad_keys, grad_values, grad_gate = outs
    return gated, grad_queries, grad_keys, grad_values, grad_gate.reshape(-1)


def solution(mesh):
    text, latents = P("seq", "vis"), P("seq", "vis", None)
    return jax.shard_map(
        local,
        mesh=mesh,
        in_specs=(text, latents, latents, P("vis"), text, P(), P()),
        out_specs=(text, text, latents, latents, P("vis")),
        check_vma=False,
    )
```

```python
import math

import jax
import jax.numpy as jnp
from jax import lax
from jax.experimental import pallas as pl
from jax.experimental.pallas import tpu as pltpu
from jax.sharding import PartitionSpec as P

HD = 128
LAT = 64
PART = 16
DOC = 32
DOCS = 8
ATT = 12
BLK = 512
ROWS = 2048
HEADS = 4
BLOCKS = 8
HALF = HEADS * HD
NEAR = 32
KEYS = ATT * LAT
SCALE = 1.0 / math.sqrt(HD)
EXP_SCALE = math.log2(math.e) / math.sqrt(HD)
MESH = pl.DeviceIdType.MESH
f32, bf16, i32 = jnp.float32, jnp.bfloat16, jnp.int32


def contract_last(left, right):
    return lax.dot_general(left, right, (((1,), (1,)), ((), ())), preferred_element_type=f32)


def dot(left, right):
    return jnp.dot(left, right, preferred_element_type=f32)


def kernel(
    slot_ref, lists_ref, q_hbm, cot_hbm, lk_hbm, lv_hbm, gate_ref,
    out_hbm, gq_hbm, gk_out, gv_out, gate_out,
    own_slot, own_doc, inverse,
    lk, lv, near_send, near_recv, x_recv, q_work, c_work, k_all, v_all, k_blk, v_blk,
    k_term, v_term, bx_recv, back_send, back_recv,
    g_part, g_x, g_row, g_y, g_all,
    ns, nr, xs, xr, bxs, bxr, bs, br,
    lr, til, tis, tir, tol, tos, tor, gxs, gxr, gys, gyr, gcs, gcr,
):
    seq = lax.axis_index("seq")
    z = lax.axis_index("vis")
    c = seq % 2
    x = (seq // 2) % 4
    y = seq // 8

    def at_near(g, k):
        return (((y + g) % 4) * 8 + x * 2 + (c + k) % 2, (z + k // 2) % 4)

    def at_x(k):
        return (y * 8 + ((x + k) % 4) * 2 + c, z)

    sibling = at_near(0, 1)

    def copy(src, dst, send, recv, device, k):
        if k == 0:
            return pltpu.make_async_copy(src, dst, recv)
        return pltpu.make_async_remote_copy(
            src_ref=src, dst_ref=dst, send_sem=send, recv_sem=recv, device_id=device, device_id_type=MESH
        )

    def near_copy(h, g, k, remote):
        to_z, to_c, to_y = (z + k // 2) % 4, (c + k) % 2, (y + g) % 4
        src = near_send.at[h, to_z * 2 + to_c, pl.ds(2 * to_y, 2)]
        dst = near_recv.at[h, :, y * 2 + c, :, pl.ds(pl.multiple_of(z * PART, PART), PART), :]
        if not remote:
            return pltpu.make_async_copy(src, dst, nr.at[h, g])
        return copy(src, dst, ns.at[h, g, k], nr.at[h, g], at_near(g, k), 1)

    def x_copy(h, g, k):
        rows = 2 * ((y + 4 - g) % 4)
        return copy(
            near_recv.at[h, ((x + k) % 4) // 2, pl.ds(rows, 2)], x_recv.at[h, pl.ds(x * 8 + rows, 2)],
            xs.at[h, g, k], xr.at[h, g, k], at_x(k), k)

    def bx_copy(h, g, k):
        rows = 2 * ((y + g) % 4)
        return copy(
            x_recv.at[h, pl.ds(((x + k) % 4) * 8 + rows, 2)], bx_recv.at[h, x, pl.ds(rows, 2)],
            bxs.at[h, g, k], bxr.at[h, g, k], at_x(k), k)

    def back_copy(h, g, k, remote):
        to_z, to_c, to_y = (z + k // 2) % 4, (c + k) % 2, (y + g) % 4
        src = back_send.at[h, :, to_y, to_c, :, pl.ds(pl.multiple_of(to_z * PART, PART), PART), :]
        dst = back_recv.at[h, z * 2 + c, pl.ds(2 * y, 2)]
        if not remote:
            return pltpu.make_async_copy(src, dst, br.at[h])
        return copy(src, dst, bs.at[h, g, k], br.at[h], at_near(g, k), 1)

    def start_group(make, h, g):
        make(h, g, 0, g != 0).start()
        for k in range(1, 8):
            make(h, g, k, True).start()

    def sent_group(make, h, g):
        if g != 0:
            make(h, g, 0, True).wait_send()
        for k in range(1, 8):
            make(h, g, k, True).wait_send()

    def group_arrive(make, h, g):
        make(h, g, 0).wait()
        for k in range(1, 4):
            make(h, g, k).wait_recv()

    def group_sent(make, h, g):
        for k in range(1, 4):
            make(h, g, k).wait_send()

    def columns(half, h):
        return pl.ds(pl.multiple_of(half * HALF + h * HD, HD), HD)

    def text_local(h):
        return [
            pltpu.make_async_copy(src.at[:, columns(c, h)], dst.at[h, pl.ds(0, ROWS)], til.at[h, i])
            for i, (src, dst) in enumerate(((q_hbm, q_work), (cot_hbm, c_work)))]

    def text_remote(h):
        return [
            copy(src.at[:, columns(1 - c, h)], dst.at[h, pl.ds(ROWS, ROWS)],
                 tis.at[h, i], tir.at[h, i], sibling, 1)
            for i, (src, dst) in enumerate(((q_hbm, q_work), (cot_hbm, c_work)))]

    def result_local(h):
        return [
            pltpu.make_async_copy(src.at[h, pl.ds(0, ROWS)], dst.at[:, columns(c, h)], tol.at[h, i])
            for i, (src, dst) in enumerate(((q_work, gq_hbm), (c_work, out_hbm)))]

    def result_remote(h):
        return [
            copy(src.at[h, pl.ds(ROWS, ROWS)], dst.at[:, columns(c, h)],
                 tos.at[h, i], tor.at[h, i], sibling, 1)
            for i, (src, dst) in enumerate(((q_work, gq_hbm), (c_work, out_hbm)))]

    def start(copies):
        for one in copies:
            one.start()

    staged = [
        pltpu.make_async_copy(src, dst, lr.at[i]) for i, (src, dst) in enumerate(((lk_hbm, lk), (lv_hbm, lv)))]
    start(staged)

    @pl.loop(0, HEADS)
    def _(h):
        start(text_local(h))

    barrier = pltpu.get_barrier_semaphore()

    @pl.loop(1, NEAR)
    def _(j):
        pl.semaphore_signal(barrier, inc=1, device_id=at_near(j // 8, j % 8), device_id_type=MESH)

    for k in range(1, 4):
        pl.semaphore_signal(barrier, inc=1, device_id=at_x(k), device_id_type=MESH)

    slots = []
    for d in range(DOCS):
        def look(i, found, d=d):
            at = slot_ref[d * DOC + i]
            return found + jnp.where(at // 8 == seq, at % 8, 0)
        slots.append(lax.fori_loop(0, DOC, look, jnp.int32(0), unroll=True))
        own_slot[d] = slots[d]
    for j in range(DOCS):
        doc = jnp.int32(0)
        for d in range(DOCS):
            doc = jnp.where(slots[d] == j, d, doc)
        own_doc[j] = doc

    for one in staged:
        one.wait()

    @pl.loop(0, DOCS)
    def _(d):
        at = own_slot[d]
        for i, src in enumerate((lk, lv)):
            row = src[at]
            for to in range(8):
                for h in range(HEADS):
                    low = (to * HEADS + h) * HD
                    near_send[h, to, d, i] = row[:, low:low + HD]

    pl.semaphore_wait(barrier, NEAR - 1 + 3)

    def send_out(h):
        for g in (0, 1, 3, 2):
            start_group(near_copy, h, g)

    def block_row(b):
        own = seq * 4 + b
        return jnp.where(b < 4, own, (seq + 1 - 2 * c) * 4 + b - 4)

    def place(b, a):
        owner = slot_ref[lists_ref[a, block_row(b)]] // 8
        return ((owner // 2) % 4) * 8 + (owner // 8) * 2 + owner % 2

    def pass_group(h, g):
        rows = near_recv.at[h, :, pl.ds(2 * ((y + 4 - g) % 4), 2)]
        pltpu.make_async_copy(rows, rows, nr.at[h, g]).wait()
        start([x_copy(h, g, k) for k in range(4)])

    def pass_on(h):
        for g in (0, 1, 3, 2):
            pass_group(h, g)

    start_group(near_copy, 0, 0)
    start_group(near_copy, 0, 1)
    pass_group(0, 0)
    start_group(near_copy, 0, 3)
    pass_group(0, 1)
    start_group(near_copy, 0, 2)
    start(text_remote(0))
    pass_group(0, 3)
    pass_group(0, 2)
    send_out(1)

    @pl.loop(1, HEADS)
    def _(h):
        start(text_remote(h))

    @pl.loop(0, BLOCKS)
    def _(b):
        places = [place(b, a) for a in range(ATT)]

        @pl.loop(0, DOC)
        def _(p):
            found = jnp.int32(ATT)
            for a in range(ATT):
                found = jnp.where(places[a] == p, a, found)
            inverse[b, p] = found

    k_term[:, ATT] = jnp.zeros((BLOCKS, LAT, HD), f32)
    v_term[:, ATT] = jnp.zeros((BLOCKS, LAT, HD), f32)
    v_blk[:, HD:] = jnp.ones((KEYS, HD), bf16)
    g_part[...] = jnp.zeros((8, HD), f32)

    def fold_group(h, g):
        group_arrive(bx_copy, h, g)
        to_y = (y + g) % 4
        for i in range(2):
            for p in range(2):
                both = bx_recv[h, 2 * p, 2 * to_y + i].astype(f32) + bx_recv[h, 2 * p + 1, 2 * to_y + i].astype(f32)
                back_send[h, p, to_y, i] = both.astype(bf16)
        start_group(back_copy, h, g)

    def return_group(h, g):
        start([bx_copy(h, g, k) for k in range(4)])

    def fold(h):
        for g in (2, 1, 3, 0):
            fold_group(h, g)

    @pl.loop(0, HEADS)
    def _(h):
        for g in range(4):
            group_arrive(x_copy, h, g)
        for one in text_local(h):
            one.wait()
        for one in text_remote(h):
            one.wait_recv()
        k_all[...] = x_recv[h, :, 0]
        v_all[...] = x_recv[h, :, 1]
        gate = jnp.tanh(gate_ref[c * HEADS + h])

        def block(b, total):
            @pl.when((h == 0) & (b == 0))
            def _():
                pass_on(1)
                send_out(2)

            @pl.when((h == 0) & (b == 3))
            def _():
                send_out(3)

            @pl.when((h == 0) & (b == 5))
            def _():
                pass_on(2)

            @pl.when((h == 1) & (b == 3))
            def _():
                pass_on(3)

            @pl.when((h >= 2) & (b == 3))
            def _():
                fold(h - 2)

            for a in range(ATT):
                at = place(b, a)
                k_blk[a * LAT:(a + 1) * LAT] = k_all[at]
                v_blk[a * LAT:(a + 1) * LAT, :HD] = v_all[at]
            keys = k_blk[...]
            values = v_blk[...]
            rows = pl.ds(pl.multiple_of(b * BLK, BLK), BLK)
            queries = q_work[h, rows]
            cot = c_work[h, rows].astype(f32)
            grad_attn = (cot * gate).astype(bf16)
            scores = contract_last(queries, keys)
            top = jnp.max(scores, axis=1, keepdims=True)
            raised = jnp.exp2((scores - top) * EXP_SCALE)
            raised_low = raised.astype(bf16)
            summed = dot(raised_low, values)
            share = 1.0 / summed[:, HD:]
            attended = summed[:, :HD] * share
            c_work[h, rows] = (attended * gate).astype(bf16)
            total = total + jnp.sum((cot * attended).reshape(BLK // 8, 8, HD), axis=0)
            row_dot = jnp.sum(grad_attn.astype(f32) * attended, axis=1, keepdims=True)
            grad_weights = contract_last(grad_attn, values[:, :HD])
            grad_scores = (raised * (grad_weights - row_dot)).astype(bf16)
            scaled = share * SCALE
            q_work[h, rows] = (dot(grad_scores, keys) * scaled).astype(bf16)
            query_share = (queries.astype(f32) * scaled).astype(bf16)
            grad_share = (grad_attn.astype(f32) * share).astype(bf16)
            k_term[b, :ATT] = dot(query_share.T, grad_scores).T.reshape(ATT, LAT, HD)
            v_term[b, :ATT] = dot(grad_share.T, raised_low).T.reshape(ATT, LAT, HD)
            return total

        total = lax.fori_loop(0, BLOCKS, block, jnp.zeros((8, HD), f32), unroll=UNROLL)
        g_part[pl.ds(h, 1)] = jnp.sum(total, axis=0, keepdims=True) * (1.0 - gate * gate)

        start(result_local(h))
        start(result_remote(h))

        @pl.loop(0, DOC)
        def _(p):
            key_sum = k_term[0, inverse[0, p]]
            value_sum = v_term[0, inverse[0, p]]
            for b in range(1, BLOCKS):
                key_sum = key_sum + k_term[b, inverse[b, p]]
                value_sum = value_sum + v_term[b, inverse[b, p]]
            x_recv[h, p, 0] = key_sum.astype(bf16)
            x_recv[h, p, 1] = value_sum.astype(bf16)

        return_group(h, 2)
        return_group(h, 1)

        @pl.when(h < HEADS - 1)
        def _():
            return_group(h, 3)
            return_group(h, 0)

    def gx_copy(k):
        return copy(g_part, g_x.at[x], gxs.at[k], gxr.at[k], at_x(k), k)

    def gy_copy(k):
        return copy(g_row, g_y.at[y], gys.at[k], gyr.at[k], at_near(k, 0), k)

    def gc_copy(k):
        return copy(g_row, g_all.at[c], gcs.at[k], gcr.at[k], sibling, k)

    def settle_x():
        for k in range(4):
            gx_copy(k).wait()
        g_row[...] = (g_x[0] + g_x[1]) + (g_x[2] + g_x[3])
        start([gy_copy(k) for k in range(4)])

    def settle_y():
        for k in range(4):
            gy_copy(k).wait()
        g_row[...] = (g_y[0] + g_y[1]) + (g_y[2] + g_y[3])
        start([gc_copy(k) for k in range(2)])

    last = HEADS - 1
    start([gx_copy(k) for k in range(4)])
    fold(last - 1)
    fold_group(last, 2)
    return_group(last, 3)
    fold_group(last, 1)
    return_group(last, 0)
    settle_x()
    fold_group(last, 3)
    settle_y()
    fold_group(last, 0)

    @pl.loop(0, HEADS)
    def _(h):
        for g in range(4):
            sent_group(near_copy, h, g)
            group_sent(x_copy, h, g)
        for one in text_remote(h):
            one.wait_send()

    @pl.loop(0, HEADS)
    def _(h):
        for one in result_local(h):
            one.wait()
        for one in result_remote(h):
            one.wait()

    gc_copy(0).wait()
    gc_copy(1).wait()
    for half in range(2):
        gate_out[half * HEADS:(half + 1) * HEADS] = g_all[half, :HEADS]

    @pl.loop(0, HEADS)
    def _(h):
        for g in range(4):
            group_sent(bx_copy, h, g)
            sent_group(back_copy, h, g)
        pltpu.make_async_copy(back_recv.at[h], back_recv.at[h], br.at[h]).wait()

    @pl.loop(0, DOCS)
    def _(j):
        d = own_doc[j]
        for h in range(HEADS):
            for source in range(8):
                low = (source * HEADS + h) * HD
                gk_out[j, :, low:low + HD] = back_recv[h, source, d, 0]
                gv_out[j, :, low:low + HD] = back_recv[h, source, d, 1]


UNROLL = 1
VMEM = 48


def local(queries, latent_keys, latent_values, gate_vector, cotangent, image_slot, image_lists):
    smem = pl.BlockSpec(memory_space=pltpu.SMEM)
    vmem = pl.BlockSpec(memory_space=pltpu.VMEM)
    hbm = pl.BlockSpec(memory_space=pl.ANY)
    dma = pltpu.SemaphoreType.DMA
    outs = pl.pallas_call(
        kernel,
        out_shape=[
            pltpu.VMEM(queries.shape, bf16),
            pltpu.VMEM(queries.shape, bf16),
            pltpu.VMEM(latent_keys.shape, bf16),
            pltpu.VMEM(latent_keys.shape, bf16),
            pltpu.VMEM((2 * HEADS, HD), f32),
        ],
        in_specs=[smem, smem, hbm, hbm, hbm, hbm, vmem],
        out_specs=[vmem, vmem, vmem, vmem, vmem],
        scratch_shapes=[
            pltpu.SMEM((DOCS,), i32),
            pltpu.SMEM((DOCS,), i32),
            pltpu.SMEM((BLOCKS, DOC), i32),
            pltpu.VMEM((DOCS, PART, 8 * HALF), bf16),
            pltpu.VMEM((DOCS, PART, 8 * HALF), bf16),
            pltpu.VMEM((HEADS, 8, DOCS, 2, PART, HD), bf16),
            pltpu.VMEM((HEADS, 2, 8, 2, LAT, HD), bf16),
            pltpu.VMEM((HEADS, DOC, 2, LAT, HD), bf16),
            pltpu.VMEM((HEADS, 2 * ROWS, HD), bf16),
            pltpu.VMEM((HEADS, 2 * ROWS, HD), bf16),
            pltpu.VMEM((DOC, LAT, HD), bf16),
            pltpu.VMEM((DOC, LAT, HD), bf16),
            pltpu.VMEM((KEYS, HD), bf16),
            pltpu.VMEM((KEYS, 2 * HD), bf16),
            pltpu.VMEM((BLOCKS, ATT + 1, LAT, HD), f32),
            pltpu.VMEM((BLOCKS, ATT + 1, LAT, HD), f32),
            pltpu.VMEM((HEADS, 4, 8, 2, LAT, HD), bf16),
            pltpu.VMEM((HEADS, 2, 4, 2, 2, LAT, HD), bf16),
            pltpu.VMEM((HEADS, 8, DOCS, 2, PART, HD), bf16),
            pltpu.VMEM((8, HD), f32),
            pltpu.VMEM((4, 8, HD), f32),
            pltpu.VMEM((8, HD), f32),
            pltpu.VMEM((4, 8, HD), f32),
            pltpu.VMEM((2, 8, HD), f32),
            dma((HEADS, 4, 8)), dma((HEADS, 4)), dma((HEADS, 4, 4)), dma((HEADS, 4, 4)),
            dma((HEADS, 4, 4)), dma((HEADS, 4, 4)), dma((HEADS, 4, 8)), dma((HEADS,)),
            dma((2,)), dma((HEADS, 2)), dma((HEADS, 2)), dma((HEADS, 2)), dma((HEADS, 2)), dma((HEADS, 2)), dma((HEADS, 2)),
            dma((4,)), dma((4,)), dma((4,)), dma((4,)), dma((2,)), dma((2,)),
        ],
        compiler_params=pltpu.CompilerParams(
            collective_id=0, has_side_effects=True, vmem_limit_bytes=VMEM * 2**20
        ),
        name="attention",
    )(image_slot, image_lists.T, queries, cotangent, latent_keys, latent_values, gate_vector.reshape(2 * HEADS, 1, HD))
    gated, grad_queries, grad_keys, grad_values, grad_gate = outs
    return gated, grad_queries, grad_keys, grad_values, grad_gate.reshape(-1)


def solution(mesh):
    text, latents = P("seq", "vis"), P("seq", "vis", None)
    return jax.shard_map(
        local,
        mesh=mesh,
        in_specs=(text, latents, latents, P("vis"), text, P(), P()),
        out_specs=(text, text, latents, latents, P("vis")),
        check_vma=False,
    )
```

```python
import math

import jax
import jax.numpy as jnp
from jax import lax
from jax.experimental import pallas as pl
from jax.experimental.pallas import tpu as pltpu
from jax.sharding import PartitionSpec as P

HD = 128
LAT = 64
PART = 16
DOC = 32
DOCS = 8
ATT = 12
BLK = 512
ROWS = 2048
HEADS = 4
BLOCKS = 8
HALF = HEADS * HD
NEAR = 32
KEYS = ATT * LAT
SCALE = 1.0 / math.sqrt(HD)
EXP_SCALE = math.log2(math.e) / math.sqrt(HD)
MESH = pl.DeviceIdType.MESH
f32, bf16, i32 = jnp.float32, jnp.bfloat16, jnp.int32


def contract_last(left, right):
    return lax.dot_general(left, right, (((1,), (1,)), ((), ())), preferred_element_type=f32)


def dot(left, right):
    return jnp.dot(left, right, preferred_element_type=f32)


def kernel(
    slot_ref, lists_ref, q_hbm, cot_hbm, lk_hbm, lv_hbm, gate_ref,
    out_hbm, gq_hbm, gk_out, gv_out, gate_out,
    own_slot, own_doc, inverse,
    lk, lv, near_send, near_recv, x_recv, q_work, c_work, k_all, v_all, k_blk, v_blk,
    k_term, v_term, bx_recv, back_send, back_recv,
    g_part, g_x, g_row, g_y, g_all,
    ns, nr, xs, xr, bxs, bxr, bs, br,
    lr, til, tis, tir, tol, tos, tor, gxs, gxr, gys, gyr, gcs, gcr,
):
    seq = lax.axis_index("seq")
    z = lax.axis_index("vis")
    c = seq % 2
    x = (seq // 2) % 4
    y = seq // 8

    def at_near(g, k):
        return (((y + g) % 4) * 8 + x * 2 + (c + k) % 2, (z + k // 2) % 4)

    def at_x(k):
        return (y * 8 + ((x + k) % 4) * 2 + c, z)

    sibling = at_near(0, 1)

    def copy(src, dst, send, recv, device, k):
        if k == 0:
            return pltpu.make_async_copy(src, dst, recv)
        return pltpu.make_async_remote_copy(
            src_ref=src, dst_ref=dst, send_sem=send, recv_sem=recv, device_id=device, device_id_type=MESH
        )

    def near_copy(h, g, k, remote):
        to_z, to_c, to_y = (z + k // 2) % 4, (c + k) % 2, (y + g) % 4
        src = near_send.at[h, to_z * 2 + to_c, pl.ds(2 * to_y, 2)]
        dst = near_recv.at[h, :, y * 2 + c, :, pl.ds(pl.multiple_of(z * PART, PART), PART), :]
        if not remote:
            return pltpu.make_async_copy(src, dst, nr.at[h, g])
        return copy(src, dst, ns.at[h, g, k if g == 0 else 0], nr.at[h, g], at_near(g, k), 1)

    def x_copy(h, g, k):
        rows = 2 * ((y + 4 - g) % 4)
        return copy(
            near_recv.at[h, ((x + k) % 4) // 2, pl.ds(rows, 2)], x_recv.at[h, pl.ds(x * 8 + rows, 2)],
            xs.at[h, g, k], xr.at[h, g, k], at_x(k), k)

    def bx_copy(h, g, k):
        rows = 2 * ((y + g) % 4)
        return copy(
            x_recv.at[h, pl.ds(((x + k) % 4) * 8 + rows, 2)], bx_recv.at[h, x, pl.ds(rows, 2)],
            bxs.at[h, g, k], bxr.at[h, g, k], at_x(k), k)

    def back_copy(h, g, k, remote):
        to_z, to_c, to_y = (z + k // 2) % 4, (c + k) % 2, (y + g) % 4
        src = back_send.at[h, :, to_y, to_c, :, pl.ds(pl.multiple_of(to_z * PART, PART), PART), :]
        dst = back_recv.at[h, z * 2 + c, pl.ds(2 * y, 2)]
        if not remote:
            return pltpu.make_async_copy(src, dst, br.at[h])
        return copy(src, dst, bs.at[h, g, k if g == 0 else 0], br.at[h], at_near(g, k), 1)

    def start_group(make, h, g):
        make(h, g, 0, g != 0).start()
        for k in range(1, 8):
            make(h, g, k, True).start()

    def sent_group(make, h, g):
        if g == 0:
            for k in range(1, 8):
                make(h, g, k, True).wait_send()
            return
        to_y = (y + g) % 4
        if make is near_copy:
            rows, done = near_send.at[h, :, pl.ds(2 * to_y, 2)], ns.at[h, g, 0]
        else:
            rows, done = back_send.at[h, :, to_y], bs.at[h, g, 0]
        pltpu.make_async_copy(rows, rows, done).wait()

    def group_arrive(make, h, g):
        make(h, g, 0).wait()
        for k in range(1, 4):
            make(h, g, k).wait_recv()

    def group_sent(make, h, g):
        for k in range(1, 4):
            make(h, g, k).wait_send()

    def columns(half, h):
        return pl.ds(pl.multiple_of(half * HALF + h * HD, HD), HD)

    def text_local(h):
        return [
            pltpu.make_async_copy(src.at[:, columns(c, h)], dst.at[h, pl.ds(0, ROWS)], til.at[h, i])
            for i, (src, dst) in enumerate(((q_hbm, q_work), (cot_hbm, c_work)))]

    def text_remote(h):
        return [
            copy(src.at[:, columns(1 - c, h)], dst.at[h, pl.ds(ROWS, ROWS)],
                 tis.at[h, i], tir.at[h, i], sibling, 1)
            for i, (src, dst) in enumerate(((q_hbm, q_work), (cot_hbm, c_work)))]

    def result_local(h):
        return [
            pltpu.make_async_copy(src.at[h, pl.ds(0, ROWS)], dst.at[:, columns(c, h)], tol.at[h, i])
            for i, (src, dst) in enumerate(((q_work, gq_hbm), (c_work, out_hbm)))]

    def result_remote(h):
        return [
            copy(src.at[h, pl.ds(ROWS, ROWS)], dst.at[:, columns(c, h)],
                 tos.at[h, i], tor.at[h, i], sibling, 1)
            for i, (src, dst) in enumerate(((q_work, gq_hbm), (c_work, out_hbm)))]

    def start(copies):
        for one in copies:
            one.start()

    barrier = pltpu.get_barrier_semaphore()

    @pl.loop(1, NEAR)
    def _(j):
        pl.semaphore_signal(barrier, inc=1, device_id=at_near(j // 8, j % 8), device_id_type=MESH)

    for k in range(1, 4):
        pl.semaphore_signal(barrier, inc=1, device_id=at_x(k), device_id_type=MESH)

    staged = [
        pltpu.make_async_copy(src, dst, lr.at[i]) for i, (src, dst) in enumerate(((lk_hbm, lk), (lv_hbm, lv)))]
    start(staged)

    @pl.loop(0, HEADS)
    def _(h):
        start(text_local(h))

    slots = []
    for d in range(DOCS):
        def look(i, found, d=d):
            at = slot_ref[d * DOC + i]
            return found + jnp.where(at // 8 == seq, at % 8, 0)
        slots.append(lax.fori_loop(0, DOC, look, jnp.int32(0), unroll=True))
        own_slot[d] = slots[d]
    for j in range(DOCS):
        doc = jnp.int32(0)
        for d in range(DOCS):
            doc = jnp.where(slots[d] == j, d, doc)
        own_doc[j] = doc

    for one in staged:
        one.wait()

    @pl.loop(0, DOCS)
    def _(d):
        at = own_slot[d]
        for i, src in enumerate((lk, lv)):
            row = src[at]
            for to in range(8):
                for h in range(HEADS):
                    low = (to * HEADS + h) * HD
                    near_send[h, to, d, i] = row[:, low:low + HD]

    pl.semaphore_wait(barrier, NEAR - 1 + 3)

    def send_out(h):
        for g in (0, 1, 3, 2):
            start_group(near_copy, h, g)

    def block_row(b):
        own = seq * 4 + b
        return jnp.where(b < 4, own, (seq + 1 - 2 * c) * 4 + b - 4)

    def place(b, a):
        owner = slot_ref[lists_ref[a, block_row(b)]] // 8
        return ((owner // 2) % 4) * 8 + (owner // 8) * 2 + owner % 2

    def pass_group(h, g):
        rows = near_recv.at[h, :, pl.ds(2 * ((y + 4 - g) % 4), 2)]
        pltpu.make_async_copy(rows, rows, nr.at[h, g]).wait()
        start([x_copy(h, g, k) for k in range(4)])

    def pass_on(h):
        for g in (0, 1, 3, 2):
            pass_group(h, g)

    start_group(near_copy, 0, 0)
    start_group(near_copy, 0, 1)
    pass_group(0, 0)
    start_group(near_copy, 0, 3)
    pass_group(0, 1)
    start_group(near_copy, 0, 2)
    start(text_remote(0))
    pass_group(0, 3)
    pass_group(0, 2)
    send_out(1)

    @pl.loop(1, HEADS)
    def _(h):
        start(text_remote(h))

    @pl.loop(0, BLOCKS)
    def _(b):
        places = [place(b, a) for a in range(ATT)]

        @pl.loop(0, DOC)
        def _(p):
            found = jnp.int32(ATT)
            for a in range(ATT):
                found = jnp.where(places[a] == p, a, found)
            inverse[b, p] = found

    k_term[:, ATT] = jnp.zeros((BLOCKS, LAT, HD), f32)
    v_term[:, ATT] = jnp.zeros((BLOCKS, LAT, HD), f32)
    v_blk[:, HD:] = jnp.ones((KEYS, HD), bf16)
    g_part[...] = jnp.zeros((8, HD), f32)

    def fold_group(h, g):
        group_arrive(bx_copy, h, g)
        to_y = (y + g) % 4
        for i in range(2):
            for p in range(2):
                both = bx_recv[h, 2 * p, 2 * to_y + i].astype(f32) + bx_recv[h, 2 * p + 1, 2 * to_y + i].astype(f32)
                back_send[h, p, to_y, i] = both.astype(bf16)
        start_group(back_copy, h, g)

    def return_group(h, g):
        start([bx_copy(h, g, k) for k in range(4)])

    def fold(h):
        for g in (2, 1, 3, 0):
            fold_group(h, g)

    group_arrive(x_copy, 0, 0)
    group_arrive(x_copy, 0, 1)
    pass_group(1, 0)
    group_arrive(x_copy, 0, 3)
    pass_group(1, 1)

    @pl.loop(0, HEADS)
    def _(h):
        @pl.when(h > 0)
        def _():
            for g in (0, 1, 3):
                group_arrive(x_copy, h, g)

        group_arrive(x_copy, h, 2)
        for one in text_local(h):
            one.wait()
        for one in text_remote(h):
            one.wait_recv()
        k_all[...] = x_recv[h, :, 0]
        v_all[...] = x_recv[h, :, 1]
        gate = jnp.tanh(gate_ref[c * HEADS + h])

        def block(b, total):
            @pl.when((h == 0) & (b == 0))
            def _():
                pass_group(1, 3)
                pass_group(1, 2)
                send_out(2)

            @pl.when((h == 0) & (b == 3))
            def _():
                send_out(3)

            @pl.when((h == 0) & (b == 5))
            def _():
                pass_on(2)

            @pl.when((h == 1) & (b == 3))
            def _():
                pass_on(3)

            @pl.when((h >= 2) & (b == 5))
            def _():
                fold(h - 2)

            for a in range(ATT):
                at = place(b, a)
                k_blk[a * LAT:(a + 1) * LAT] = k_all[at]
                v_blk[a * LAT:(a + 1) * LAT, :HD] = v_all[at]
            keys = k_blk[...]
            values = v_blk[...]
            rows = pl.ds(pl.multiple_of(b * BLK, BLK), BLK)
            queries = q_work[h, rows]
            cot = c_work[h, rows].astype(f32)
            grad_attn = (cot * gate).astype(bf16)
            scores = contract_last(queries, keys)
            top = jnp.max(scores, axis=1, keepdims=True)
            raised = jnp.exp2((scores - top) * EXP_SCALE)
            raised_low = raised.astype(bf16)
            summed = dot(raised_low, values)
            share = 1.0 / summed[:, HD:]
            attended = summed[:, :HD] * share
            c_work[h, rows] = (attended * gate).astype(bf16)
            total = total + jnp.sum((cot * attended).reshape(BLK // 8, 8, HD), axis=0)
            row_dot = jnp.sum(grad_attn.astype(f32) * attended, axis=1, keepdims=True)
            grad_weights = contract_last(grad_attn, values[:, :HD])
            grad_scores = (raised * (grad_weights - row_dot)).astype(bf16)
            scaled = share * SCALE
            q_work[h, rows] = (dot(grad_scores, keys) * scaled).astype(bf16)
            query_share = (queries.astype(f32) * scaled).astype(bf16)
            grad_share = (grad_attn.astype(f32) * share).astype(bf16)
            k_term[b, :ATT] = dot(query_share.T, grad_scores).T.reshape(ATT, LAT, HD)
            v_term[b, :ATT] = dot(grad_share.T, raised_low).T.reshape(ATT, LAT, HD)
            return total

        total = lax.fori_loop(0, BLOCKS, block, jnp.zeros((8, HD), f32), unroll=UNROLL)
        g_part[pl.ds(h, 1)] = jnp.sum(total, axis=0, keepdims=True) * (1.0 - gate * gate)

        def add_up(g):
            @pl.loop(0, 8)
            def _(i):
                p = (i // 2) * 8 + 2 * ((y + g) % 4) + i % 2
                key_sum = k_term[0, inverse[0, p]]
                value_sum = v_term[0, inverse[0, p]]
                for b in range(1, BLOCKS):
                    key_sum = key_sum + k_term[b, inverse[b, p]]
                    value_sum = value_sum + v_term[b, inverse[b, p]]
                x_recv[h, p, 0] = key_sum.astype(bf16)
                x_recv[h, p, 1] = value_sum.astype(bf16)

        add_up(2)
        return_group(h, 2)
        add_up(1)
        return_group(h, 1)
        add_up(3)

        @pl.when(h < HEADS - 1)
        def _():
            return_group(h, 3)

        add_up(0)

        @pl.when(h < HEADS - 1)
        def _():
            return_group(h, 0)

        start(result_local(h))
        start(result_remote(h))

    def gx_copy(k):
        return copy(g_part, g_x.at[x], gxs.at[k], gxr.at[k], at_x(k), k)

    def gy_copy(k):
        return copy(g_row, g_y.at[y], gys.at[k], gyr.at[k], at_near(k, 0), k)

    def gc_copy(k):
        return copy(g_row, g_all.at[c], gcs.at[k], gcr.at[k], sibling, k)

    def settle_x():
        for k in range(4):
            gx_copy(k).wait()
        g_row[...] = (g_x[0] + g_x[1]) + (g_x[2] + g_x[3])
        start([gy_copy(k) for k in range(4)])

    def settle_y():
        for k in range(4):
            gy_copy(k).wait()
        g_row[...] = (g_y[0] + g_y[1]) + (g_y[2] + g_y[3])
        start([gc_copy(k) for k in range(2)])

    last = HEADS - 1
    start([gx_copy(k) for k in range(4)])
    fold(last - 1)

    @pl.loop(0, HEADS)
    def _(h):
        for g in range(4):
            sent_group(near_copy, h, g)
            group_sent(x_copy, h, g)
        for one in text_remote(h):
            one.wait_send()

    @pl.loop(0, last)
    def _(h):
        for g in range(4):
            group_sent(bx_copy, h, g)

    fold_group(last, 2)
    return_group(last, 3)
    fold_group(last, 1)
    return_group(last, 0)
    settle_x()
    fold_group(last, 3)
    settle_y()

    @pl.loop(0, last)
    def _(h):
        for g in range(4):
            sent_group(back_copy, h, g)

    fold_group(last, 0)

    @pl.loop(0, HEADS)
    def _(h):
        for one in result_local(h):
            one.wait()
        for one in result_remote(h):
            one.wait()

    for g in range(4):
        group_sent(bx_copy, last, g)
        sent_group(back_copy, last, g)

    @pl.loop(0, HEADS)
    def _(h):
        pltpu.make_async_copy(back_recv.at[h], back_recv.at[h], br.at[h]).wait()

    gc_copy(0).wait()
    gc_copy(1).wait()
    for half in range(2):
        gate_out[half * HEADS:(half + 1) * HEADS] = g_all[half, :HEADS]

    @pl.loop(0, DOCS)
    def _(j):
        d = own_doc[j]
        for h in range(HEADS):
            for source in range(8):
                low = (source * HEADS + h) * HD
                gk_out[j, :, low:low + HD] = back_recv[h, source, d, 0]
                gv_out[j, :, low:low + HD] = back_recv[h, source, d, 1]


UNROLL = 1
VMEM = 48


def deliver(*refs):
    count = len(refs) // 2
    done = refs[-1]
    copies = [pltpu.make_async_copy(refs[i], refs[count + i], done.at[i]) for i in range(count)]
    for one in copies:
        one.start()
    for one in copies:
        one.wait()


def delivered(arrays):
    anywhere = pl.BlockSpec(memory_space=pl.ANY)
    return pl.pallas_call(
        deliver,
        in_specs=[anywhere] * len(arrays),
        out_specs=[anywhere] * len(arrays),
        out_shape=[pltpu.HBM(one.shape, one.dtype) for one in arrays],
        scratch_shapes=[pltpu.SemaphoreType.DMA((len(arrays),))],
        compiler_params=pltpu.CompilerParams(vmem_limit_bytes=2**20),
        name="deliver",
    )(*[pltpu.with_memory_space_constraint(one, pltpu.VMEM) for one in arrays])


def local(queries, latent_keys, latent_values, gate_vector, cotangent, image_slot, image_lists):
    smem = pl.BlockSpec(memory_space=pltpu.SMEM)
    vmem = pl.BlockSpec(memory_space=pltpu.VMEM)
    hbm = pl.BlockSpec(memory_space=pl.ANY)
    dma = pltpu.SemaphoreType.DMA
    outs = pl.pallas_call(
        kernel,
        out_shape=[
            pltpu.VMEM(queries.shape, bf16),
            pltpu.VMEM(queries.shape, bf16),
            pltpu.VMEM(latent_keys.shape, bf16),
            pltpu.VMEM(latent_keys.shape, bf16),
            pltpu.VMEM((2 * HEADS, HD), f32),
        ],
        in_specs=[smem, smem, hbm, hbm, hbm, hbm, vmem],
        out_specs=[vmem, vmem, vmem, vmem, vmem],
        scratch_shapes=[
            pltpu.SMEM((DOCS,), i32),
            pltpu.SMEM((DOCS,), i32),
            pltpu.SMEM((BLOCKS, DOC), i32),
            pltpu.VMEM((DOCS, PART, 8 * HALF), bf16),
            pltpu.VMEM((DOCS, PART, 8 * HALF), bf16),
            pltpu.VMEM((HEADS, 8, DOCS, 2, PART, HD), bf16),
            pltpu.VMEM((HEADS, 2, 8, 2, LAT, HD), bf16),
            pltpu.VMEM((HEADS, DOC, 2, LAT, HD), bf16),
            pltpu.VMEM((HEADS, 2 * ROWS, HD), bf16),
            pltpu.VMEM((HEADS, 2 * ROWS, HD), bf16),
            pltpu.VMEM((DOC, LAT, HD), bf16),
            pltpu.VMEM((DOC, LAT, HD), bf16),
            pltpu.VMEM((KEYS, HD), bf16),
            pltpu.VMEM((KEYS, 2 * HD), bf16),
            pltpu.VMEM((BLOCKS, ATT + 1, LAT, HD), f32),
            pltpu.VMEM((BLOCKS, ATT + 1, LAT, HD), f32),
            pltpu.VMEM((HEADS, 4, 8, 2, LAT, HD), bf16),
            pltpu.VMEM((HEADS, 2, 4, 2, 2, LAT, HD), bf16),
            pltpu.VMEM((HEADS, 8, DOCS, 2, PART, HD), bf16),
            pltpu.VMEM((8, HD), f32),
            pltpu.VMEM((4, 8, HD), f32),
            pltpu.VMEM((8, HD), f32),
            pltpu.VMEM((4, 8, HD), f32),
            pltpu.VMEM((2, 8, HD), f32),
            dma((HEADS, 4, 8)), dma((HEADS, 4)), dma((HEADS, 4, 4)), dma((HEADS, 4, 4)),
            dma((HEADS, 4, 4)), dma((HEADS, 4, 4)), dma((HEADS, 4, 8)), dma((HEADS,)),
            dma((2,)), dma((HEADS, 2)), dma((HEADS, 2)), dma((HEADS, 2)), dma((HEADS, 2)), dma((HEADS, 2)), dma((HEADS, 2)),
            dma((4,)), dma((4,)), dma((4,)), dma((4,)), dma((2,)), dma((2,)),
        ],
        compiler_params=pltpu.CompilerParams(
            collective_id=0, has_side_effects=True, vmem_limit_bytes=VMEM * 2**20
        ),
        name="attention",
    )(image_slot, image_lists.T, queries, cotangent, latent_keys, latent_values, gate_vector.reshape(2 * HEADS, 1, HD))
    gated, grad_queries, grad_keys, grad_values, grad_gate = delivered(outs)
    return gated, grad_queries, grad_keys, grad_values, grad_gate.reshape(-1)


def solution(mesh):
    text, latents = P("seq", "vis"), P("seq", "vis", None)
    return jax.shard_map(
        local,
        mesh=mesh,
        in_specs=(text, latents, latents, P("vis"), text, P(), P()),
        out_specs=(text, text, latents, latents, P("vis")),
        check_vma=False,
    )
```

```python
import math

import jax
import jax.numpy as jnp
from jax import lax
from jax.experimental import pallas as pl
from jax.experimental.pallas import tpu as pltpu
from jax.sharding import PartitionSpec as P

HD = 128
LAT = 64
PART = 16
DOC = 32
DOCS = 8
ATT = 12
BLK = 512
ROWS = 2048
HEADS = 4
BLOCKS = 8
HALF = HEADS * HD
NEAR = 32
KEYS = ATT * LAT
SCALE = 1.0 / math.sqrt(HD)
EXP_SCALE = math.log2(math.e) / math.sqrt(HD)
MESH = pl.DeviceIdType.MESH
f32, bf16, i32 = jnp.float32, jnp.bfloat16, jnp.int32


def contract_last(left, right):
    return lax.dot_general(left, right, (((1,), (1,)), ((), ())), preferred_element_type=f32)


def dot(left, right):
    return jnp.dot(left, right, preferred_element_type=f32)


def kernel(
    slot_ref, lists_ref, q_hbm, cot_hbm, lk_hbm, lv_hbm, gate_ref,
    out_hbm, gq_hbm, gk_out, gv_out, gate_out,
    own_slot, own_doc, inverse,
    lk, lv, near_send, near_recv, x_recv, q_work, c_work, k_all, v_all, k_blk, v_blk,
    k_term, v_term, bx_recv, back_send, back_recv,
    g_part, g_x, g_row, g_y, g_all,
    ns, nr, xs, xr, bxs, bxr, bs, br,
    lr, til, tis, tir, tol, tos, tor, gxs, gxr, gys, gyr, gcs, gcr,
):
    seq = lax.axis_index("seq")
    z = lax.axis_index("vis")
    c = seq % 2
    x = (seq // 2) % 4
    y = seq // 8

    def at_near(g, k):
        return (((y + g) % 4) * 8 + x * 2 + (c + k) % 2, (z + k // 2) % 4)

    def at_x(k):
        return (y * 8 + ((x + k) % 4) * 2 + c, z)

    sibling = at_near(0, 1)

    def copy(src, dst, send, recv, device, k):
        if k == 0:
            return pltpu.make_async_copy(src, dst, recv)
        return pltpu.make_async_remote_copy(
            src_ref=src, dst_ref=dst, send_sem=send, recv_sem=recv, device_id=device, device_id_type=MESH
        )

    def near_copy(h, g, k, remote):
        to_z, to_c, to_y = (z + k // 2) % 4, (c + k) % 2, (y + g) % 4
        src = near_send.at[h, to_z * 2 + to_c, pl.ds(2 * to_y, 2)]
        dst = near_recv.at[h, :, y * 2 + c, :, pl.ds(pl.multiple_of(z * PART, PART), PART), :]
        if not remote:
            return pltpu.make_async_copy(src, dst, nr.at[h, g])
        return copy(src, dst, ns.at[h, g, k if g == 0 else 0], nr.at[h, g], at_near(g, k), 1)

    def x_copy(h, g, k):
        rows = 2 * ((y + 4 - g) % 4)
        return copy(
            near_recv.at[h, ((x + k) % 4) // 2, pl.ds(rows, 2)], x_recv.at[h, pl.ds(x * 8 + rows, 2)],
            xs.at[h, g, k], xr.at[h, g, k], at_x(k), k)

    def bx_copy(h, g, k):
        rows = 2 * ((y + g) % 4)
        return copy(
            x_recv.at[h, pl.ds(((x + k) % 4) * 8 + rows, 2)], bx_recv.at[h, x, pl.ds(rows, 2)],
            bxs.at[h, g, k], bxr.at[h, g, k], at_x(k), k)

    def back_copy(h, g, k, remote):
        to_z, to_c, to_y = (z + k // 2) % 4, (c + k) % 2, (y + g) % 4
        src = back_send.at[h, :, to_y, to_c, :, pl.ds(pl.multiple_of(to_z * PART, PART), PART), :]
        dst = back_recv.at[h, z * 2 + c, pl.ds(2 * y, 2)]
        if not remote:
            return pltpu.make_async_copy(src, dst, br.at[h])
        return copy(src, dst, bs.at[h, g, k if g == 0 else 0], br.at[h], at_near(g, k), 1)

    def start_group(make, h, g):
        make(h, g, 0, g != 0).start()
        for k in range(1, 8):
            make(h, g, k, True).start()

    def sent_group(make, h, g):
        if g == 0:
            for k in range(1, 8):
                make(h, g, k, True).wait_send()
            return
        to_y = (y + g) % 4
        if make is near_copy:
            rows, done = near_send.at[h, :, pl.ds(2 * to_y, 2)], ns.at[h, g, 0]
        else:
            rows, done = back_send.at[h, :, to_y], bs.at[h, g, 0]
        pltpu.make_async_copy(rows, rows, done).wait()

    def group_arrive(make, h, g):
        make(h, g, 0).wait()
        for k in range(1, 4):
            make(h, g, k).wait_recv()

    def group_sent(make, h, g):
        for k in range(1, 4):
            make(h, g, k).wait_send()

    def columns(half, h):
        return pl.ds(pl.multiple_of(half * HALF + h * HD, HD), HD)

    def text_local(h):
        return [
            pltpu.make_async_copy(src.at[:, columns(c, h)], dst.at[h, pl.ds(0, ROWS)], til.at[h, i])
            for i, (src, dst) in enumerate(((q_hbm, q_work), (cot_hbm, c_work)))]

    def text_remote(h):
        return [
            copy(src.at[:, columns(1 - c, h)], dst.at[h, pl.ds(ROWS, ROWS)],
                 tis.at[h, i], tir.at[h, i], sibling, 1)
            for i, (src, dst) in enumerate(((q_hbm, q_work), (cot_hbm, c_work)))]

    def result_local(h):
        return [
            pltpu.make_async_copy(src.at[h, pl.ds(0, ROWS)], dst.at[:, columns(c, h)], tol.at[h, i])
            for i, (src, dst) in enumerate(((q_work, gq_hbm), (c_work, out_hbm)))]

    def result_remote(h):
        return [
            copy(src.at[h, pl.ds(ROWS, ROWS)], dst.at[:, columns(c, h)],
                 tos.at[h, i], tor.at[h, i], sibling, 1)
            for i, (src, dst) in enumerate(((q_work, gq_hbm), (c_work, out_hbm)))]

    def start(copies):
        for one in copies:
            one.start()

    staged = [
        pltpu.make_async_copy(src, dst, lr.at[i]) for i, (src, dst) in enumerate(((lk_hbm, lk), (lv_hbm, lv)))]
    start(staged)

    barrier = pltpu.get_barrier_semaphore()

    for j in range(1, NEAR):
        pl.semaphore_signal(barrier, inc=1, device_id=at_near(j // 8, j % 8), device_id_type=MESH)

    for k in range(1, 4):
        pl.semaphore_signal(barrier, inc=1, device_id=at_x(k), device_id_type=MESH)

    @pl.loop(0, HEADS)
    def _(h):
        start(text_local(h))

    slots = []
    for d in range(DOCS):
        def look(i, found, d=d):
            at = slot_ref[d * DOC + i]
            return found + jnp.where(at // 8 == seq, at % 8, 0)
        slots.append(lax.fori_loop(0, DOC, look, jnp.int32(0), unroll=True))
        own_slot[d] = slots[d]
    for j in range(DOCS):
        doc = jnp.int32(0)
        for d in range(DOCS):
            doc = jnp.where(slots[d] == j, d, doc)
        own_doc[j] = doc

    for one in staged:
        one.wait()

    @pl.loop(0, DOCS)
    def _(d):
        at = own_slot[d]
        for i, src in enumerate((lk, lv)):
            row = src[at]
            for to in range(8):
                for h in range(HEADS):
                    low = (to * HEADS + h) * HD
                    near_send[h, to, d, i] = row[:, low:low + HD]

    pl.semaphore_wait(barrier, NEAR - 1 + 3)

    def send_out(h):
        for g in (0, 1, 3, 2):
            start_group(near_copy, h, g)

    def block_row(b):
        own = seq * 4 + b
        return jnp.where(b < 4, own, (seq + 1 - 2 * c) * 4 + b - 4)

    def place(b, a):
        owner = slot_ref[lists_ref[a, block_row(b)]] // 8
        return ((owner // 2) % 4) * 8 + (owner // 8) * 2 + owner % 2

    def pass_group(h, g):
        rows = near_recv.at[h, :, pl.ds(2 * ((y + 4 - g) % 4), 2)]
        pltpu.make_async_copy(rows, rows, nr.at[h, g]).wait()
        start([x_copy(h, g, k) for k in range(4)])

    def pass_on(h):
        for g in (0, 1, 3, 2):
            pass_group(h, g)

    start_group(near_copy, 0, 0)
    start_group(near_copy, 0, 1)
    pass_group(0, 0)
    start_group(near_copy, 0, 3)
    pass_group(0, 1)
    start_group(near_copy, 0, 2)
    start(text_remote(0))
    pass_group(0, 3)
    pass_group(0, 2)
    send_out(1)

    @pl.loop(1, HEADS)
    def _(h):
        start(text_remote(h))

    @pl.loop(0, BLOCKS)
    def _(b):
        places = [place(b, a) for a in range(ATT)]

        @pl.loop(0, DOC)
        def _(p):
            found = jnp.int32(ATT)
            for a in range(ATT):
                found = jnp.where(places[a] == p, a, found)
            inverse[b, p] = found

    k_term[:, ATT] = jnp.zeros((BLOCKS, LAT, HD), f32)
    v_term[:, ATT] = jnp.zeros((BLOCKS, LAT, HD), f32)
    v_blk[:, HD:] = jnp.ones((KEYS, HD), bf16)
    g_part[...] = jnp.zeros((8, HD), f32)

    def fold_group(h, g):
        group_arrive(bx_copy, h, g)
        to_y = (y + g) % 4
        for i in range(2):
            for p in range(2):
                both = bx_recv[h, 2 * p, 2 * to_y + i].astype(f32) + bx_recv[h, 2 * p + 1, 2 * to_y + i].astype(f32)
                back_send[h, p, to_y, i] = both.astype(bf16)
        start_group(back_copy, h, g)

    def return_group(h, g):
        start([bx_copy(h, g, k) for k in range(4)])

    def fold(h):
        for g in (2, 1, 3, 0):
            fold_group(h, g)

    group_arrive(x_copy, 0, 0)
    group_arrive(x_copy, 0, 1)
    pass_group(1, 0)
    group_arrive(x_copy, 0, 3)
    pass_group(1, 1)

    @pl.loop(0, HEADS)
    def _(h):
        @pl.when(h > 0)
        def _():
            for g in (0, 1, 3):
                group_arrive(x_copy, h, g)

        group_arrive(x_copy, h, 2)
        for one in text_local(h):
            one.wait()
        for one in text_remote(h):
            one.wait_recv()
        k_all[...] = x_recv[h, :, 0]
        v_all[...] = x_recv[h, :, 1]
        gate = jnp.tanh(gate_ref[c * HEADS + h])

        def block(b, total):
            @pl.when((h == 0) & (b == 0))
            def _():
                pass_group(1, 3)
                pass_group(1, 2)
                send_out(2)

            @pl.when((h == 0) & (b == 3))
            def _():
                send_out(3)

            @pl.when((h == 0) & (b == 5))
            def _():
                pass_on(2)

            @pl.when((h == 1) & (b == 3))
            def _():
                pass_on(3)

            @pl.when((h >= 2) & (b == 5))
            def _():
                fold(h - 2)

            for a in range(ATT):
                at = place(b, a)
                k_blk[a * LAT:(a + 1) * LAT] = k_all[at]
                v_blk[a * LAT:(a + 1) * LAT, :HD] = v_all[at]
            keys = k_blk[...]
            values = v_blk[...]
            rows = pl.ds(pl.multiple_of(b * BLK, BLK), BLK)
            queries = q_work[h, rows]
            cot = c_work[h, rows].astype(f32)
            grad_attn = (cot * gate).astype(bf16)
            scores = contract_last(queries, keys)
            top = jnp.max(scores, axis=1, keepdims=True)
            raised = jnp.exp2((scores - top) * EXP_SCALE)
            raised_low = raised.astype(bf16)
            summed = dot(raised_low, values)
            share = 1.0 / summed[:, HD:]
            attended = summed[:, :HD] * share
            c_work[h, rows] = (attended * gate).astype(bf16)
            total = total + jnp.sum((cot * attended).reshape(BLK // 8, 8, HD), axis=0)
            row_dot = jnp.sum(grad_attn.astype(f32) * attended, axis=1, keepdims=True)
            grad_weights = contract_last(grad_attn, values[:, :HD])
            grad_scores = (raised * (grad_weights - row_dot)).astype(bf16)
            scaled = share * SCALE
            q_work[h, rows] = (dot(grad_scores, keys) * scaled).astype(bf16)
            query_share = (queries.astype(f32) * scaled).astype(bf16)
            grad_share = (grad_attn.astype(f32) * share).astype(bf16)
            k_term[b, :ATT] = dot(query_share.T, grad_scores).T.reshape(ATT, LAT, HD)
            v_term[b, :ATT] = dot(grad_share.T, raised_low).T.reshape(ATT, LAT, HD)
            return total

        total = lax.fori_loop(0, BLOCKS, block, jnp.zeros((8, HD), f32), unroll=UNROLL)
        g_part[pl.ds(h, 1)] = jnp.sum(total, axis=0, keepdims=True) * (1.0 - gate * gate)

        def add_up(g):
            @pl.loop(0, 8)
            def _(i):
                p = (i // 2) * 8 + 2 * ((y + g) % 4) + i % 2
                key_sum = k_term[0, inverse[0, p]]
                value_sum = v_term[0, inverse[0, p]]
                for b in range(1, BLOCKS):
                    key_sum = key_sum + k_term[b, inverse[b, p]]
                    value_sum = value_sum + v_term[b, inverse[b, p]]
                x_recv[h, p, 0] = key_sum.astype(bf16)
                x_recv[h, p, 1] = value_sum.astype(bf16)

        add_up(2)
        return_group(h, 2)
        add_up(1)
        return_group(h, 1)
        add_up(3)

        @pl.when(h < HEADS - 1)
        def _():
            return_group(h, 3)

        add_up(0)

        @pl.when(h < HEADS - 1)
        def _():
            return_group(h, 0)

        start(result_local(h))
        start(result_remote(h))

    def gx_copy(k):
        return copy(g_part, g_x.at[x], gxs.at[k], gxr.at[k], at_x(k), k)

    def gy_copy(k):
        return copy(g_row, g_y.at[y], gys.at[k], gyr.at[k], at_near(k, 0), k)

    def gc_copy(k):
        return copy(g_row, g_all.at[c], gcs.at[k], gcr.at[k], sibling, k)

    def settle_x():
        for k in range(4):
            gx_copy(k).wait()
        g_row[...] = (g_x[0] + g_x[1]) + (g_x[2] + g_x[3])
        start([gy_copy(k) for k in range(4)])

    def settle_y():
        for k in range(4):
            gy_copy(k).wait()
        g_row[...] = (g_y[0] + g_y[1]) + (g_y[2] + g_y[3])
        start([gc_copy(k) for k in range(2)])

    last = HEADS - 1
    start([gx_copy(k) for k in range(4)])
    fold(last - 1)

    @pl.loop(0, HEADS)
    def _(h):
        for g in range(4):
            sent_group(near_copy, h, g)
            group_sent(x_copy, h, g)
        for one in text_remote(h):
            one.wait_send()

    @pl.loop(0, last)
    def _(h):
        for g in range(4):
            group_sent(bx_copy, h, g)

    fold_group(last, 2)
    return_group(last, 3)
    fold_group(last, 1)
    return_group(last, 0)
    settle_x()
    fold_group(last, 3)
    settle_y()

    @pl.loop(0, last)
    def _(h):
        for g in range(4):
            sent_group(back_copy, h, g)

    fold_group(last, 0)

    @pl.loop(0, HEADS)
    def _(h):
        for one in result_local(h):
            one.wait()
        for one in result_remote(h):
            one.wait()

    for g in range(4):
        group_sent(bx_copy, last, g)
        sent_group(back_copy, last, g)

    @pl.loop(0, HEADS)
    def _(h):
        pltpu.make_async_copy(back_recv.at[h], back_recv.at[h], br.at[h]).wait()

    gc_copy(0).wait()
    gc_copy(1).wait()
    for half in range(2):
        gate_out[half * HEADS:(half + 1) * HEADS] = g_all[half, :HEADS]

    @pl.loop(0, DOCS)
    def _(j):
        d = own_doc[j]
        for h in range(HEADS):
            for source in range(8):
                low = (source * HEADS + h) * HD
                gk_out[j, :, low:low + HD] = back_recv[h, source, d, 0]
                gv_out[j, :, low:low + HD] = back_recv[h, source, d, 1]


UNROLL = 1
VMEM = 48


def deliver(*refs):
    count = len(refs) // 2
    done = refs[-1]
    copies = [pltpu.make_async_copy(refs[i], refs[count + i], done.at[i]) for i in range(count)]
    for one in copies:
        one.start()
    for one in copies:
        one.wait()


def delivered(arrays):
    anywhere = pl.BlockSpec(memory_space=pl.ANY)
    return pl.pallas_call(
        deliver,
        in_specs=[anywhere] * len(arrays),
        out_specs=[anywhere] * len(arrays),
        out_shape=[pltpu.HBM(one.shape, one.dtype) for one in arrays],
        scratch_shapes=[pltpu.SemaphoreType.DMA((len(arrays),))],
        compiler_params=pltpu.CompilerParams(vmem_limit_bytes=2**20),
        name="deliver",
    )(*[pltpu.with_memory_space_constraint(one, pltpu.VMEM) for one in arrays])


def local(queries, latent_keys, latent_values, gate_vector, cotangent, image_slot, image_lists):
    smem = pl.BlockSpec(memory_space=pltpu.SMEM)
    vmem = pl.BlockSpec(memory_space=pltpu.VMEM)
    hbm = pl.BlockSpec(memory_space=pl.ANY)
    dma = pltpu.SemaphoreType.DMA
    outs = pl.pallas_call(
        kernel,
        out_shape=[
            pltpu.VMEM(queries.shape, bf16),
            pltpu.VMEM(queries.shape, bf16),
            pltpu.VMEM(latent_keys.shape, bf16),
            pltpu.VMEM(latent_keys.shape, bf16),
            pltpu.VMEM((2 * HEADS, HD), f32),
        ],
        in_specs=[smem, smem, hbm, hbm, hbm, hbm, vmem],
        out_specs=[vmem, vmem, vmem, vmem, vmem],
        scratch_shapes=[
            pltpu.SMEM((DOCS,), i32),
            pltpu.SMEM((DOCS,), i32),
            pltpu.SMEM((BLOCKS, DOC), i32),
            pltpu.VMEM((DOCS, PART, 8 * HALF), bf16),
            pltpu.VMEM((DOCS, PART, 8 * HALF), bf16),
            pltpu.VMEM((HEADS, 8, DOCS, 2, PART, HD), bf16),
            pltpu.VMEM((HEADS, 2, 8, 2, LAT, HD), bf16),
            pltpu.VMEM((HEADS, DOC, 2, LAT, HD), bf16),
            pltpu.VMEM((HEADS, 2 * ROWS, HD), bf16),
            pltpu.VMEM((HEADS, 2 * ROWS, HD), bf16),
            pltpu.VMEM((DOC, LAT, HD), bf16),
            pltpu.VMEM((DOC, LAT, HD), bf16),
            pltpu.VMEM((KEYS, HD), bf16),
            pltpu.VMEM((KEYS, 2 * HD), bf16),
            pltpu.VMEM((BLOCKS, ATT + 1, LAT, HD), f32),
            pltpu.VMEM((BLOCKS, ATT + 1, LAT, HD), f32),
            pltpu.VMEM((HEADS, 4, 8, 2, LAT, HD), bf16),
            pltpu.VMEM((HEADS, 2, 4, 2, 2, LAT, HD), bf16),
            pltpu.VMEM((HEADS, 8, DOCS, 2, PART, HD), bf16),
            pltpu.VMEM((8, HD), f32),
            pltpu.VMEM((4, 8, HD), f32),
            pltpu.VMEM((8, HD), f32),
            pltpu.VMEM((4, 8, HD), f32),
            pltpu.VMEM((2, 8, HD), f32),
            dma((HEADS, 4, 8)), dma((HEADS, 4)), dma((HEADS, 4, 4)), dma((HEADS, 4, 4)),
            dma((HEADS, 4, 4)), dma((HEADS, 4, 4)), dma((HEADS, 4, 8)), dma((HEADS,)),
            dma((2,)), dma((HEADS, 2)), dma((HEADS, 2)), dma((HEADS, 2)), dma((HEADS, 2)), dma((HEADS, 2)), dma((HEADS, 2)),
            dma((4,)), dma((4,)), dma((4,)), dma((4,)), dma((2,)), dma((2,)),
        ],
        compiler_params=pltpu.CompilerParams(
            collective_id=0, has_side_effects=True, vmem_limit_bytes=VMEM * 2**20
        ),
        name="attention",
    )(image_slot, image_lists.T, queries, cotangent, latent_keys, latent_values, gate_vector.reshape(2 * HEADS, 1, HD))
    gated, grad_queries, grad_keys, grad_values, grad_gate = delivered(outs)
    return gated, grad_queries, grad_keys, grad_values, grad_gate.reshape(-1)


def solution(mesh):
    text, latents = P("seq", "vis"), P("seq", "vis", None)
    return jax.shard_map(
        local,
        mesh=mesh,
        in_specs=(text, latents, latents, P("vis"), text, P(), P()),
        out_specs=(text, text, latents, latents, P("vis")),
        check_vma=False,
    )
```
